32 devices in a mesh: row: 4 (over y, x), col: 8 (over z, core).
Axes of the slice: x: 2, y: 2, z: 4, core: 2. Of those that a mesh axis runs over, the one named last changes fastest.
Arguments:
- amplitudes: bfloat16 [16384, 16384], P('row', 'col'), may hold values from -6 to 6
- aux_left: bfloat16 [16384, 1024], P('col', 'row'), may hold values from -0.046875 to 0.046875
- aux_right: bfloat16 [16384, 1024], P('col', 'row'), may hold values from -0.1875 to 0.1875
- occupied_map: int32 [16384], replicated, may hold values from 0 to 63
- virtual_map: int32 [16384], replicated, may hold values from 0 to 255
- occupied_energy: float32 [64], replicated, may hold values from -3 to -0.5
- virtual_energy: float32 [256], replicated, may hold values from 0.5 to 4
Outputs:
- residual_term: float32 [16384, 16384], P('row', 'col')
The draws below stay inside these ranges and needn't reach their ends.
All inputs are finite; a program needn't handle non-finite values.
Results may differ from the reference program's by a relative error of at most 0.0029.
Values may be sent and summed in bfloat16 or wider, within the bound.
A program may use at most 192 MiB of HBM per device.

```python
import jax
import jax.numpy as jnp
from jax import lax

NO = 64
NV = 256
AUX = 1024
NT = 16384


def with_ends(array, own_key, smallest, high):
    longest = array.shape.index(max(array.shape))
    spots = []
    for shift in (0, 1):
        where = [jax.random.randint(jax.random.fold_in(own_key, axis), (), 0, length) for axis, length in enumerate(array.shape)]
        where[longest] = (where[longest] + shift) % array.shape[longest]
        spots.append(tuple(where))
    return array.at[spots[0]].set(smallest).at[spots[1]].set(high)


def level_of(own_key, dims, pieces, least, high):
    factor_of = 1.0
    for position, shards_of in pieces:
        heights = jax.random.uniform(jax.random.fold_in(jax.random.fold_in(own_key, 6), position), (shards_of,), jnp.float32, least / len(pieces), high / len(pieces))
        factor_of = factor_of * jnp.repeat(jnp.exp(heights), dims[position] // shards_of).reshape((-1,) + (1,) * (len(dims) - 1 - position))
    return factor_of


def gaussian(own_key, dims, deviation, most, shards=(), held_as=jnp.bfloat16):
    gain = level_of(own_key, dims, shards, -0.22, 0.18) if shards else 1.0
    result = jax.random.normal(own_key, dims, jnp.float32) * deviation * gain
    return jnp.minimum(jnp.maximum(result, -most), most).astype(held_as)


def setup_inputs(seed: int = 0) -> dict:
    key_of = jax.random.split(jax.random.key(seed), 8)
    return {
        "amplitudes": gaussian(key_of[0], (NT, NT), 1.0, 6.0, ((0, 4), (1, 8))),
        "aux_left": gaussian(key_of[1], (NT, AUX), NT ** -0.5, 0.046875, ((0, 8), (1, 4))),
        "aux_right": gaussian(key_of[2], (NT, AUX), AUX ** -0.5, 0.1875, ((0, 8), (1, 4))),
        "occupied_map": with_ends(jax.random.randint(key_of[3], (NT,), 0, NO), jax.random.fold_in(key_of[3], 1), 0, NO - 1).astype(jnp.int32),
        "virtual_map": with_ends(jax.random.randint(key_of[4], (NT,), 0, NV), jax.random.fold_in(key_of[4], 1), 0, NV - 1).astype(jnp.int32),
        "occupied_energy": jnp.clip(jax.random.uniform(key_of[5], (NO,), jnp.float32, -3.0, -0.5), -3.0, -0.5),
        "virtual_energy": jnp.clip(jax.random.uniform(key_of[6], (NV,), jnp.float32, 0.5, 4.0), 0.5, 4.0),
    }


def reference(amplitudes, aux_left, aux_right, occupied_map, virtual_map, occupied_energy, virtual_energy):
    fitted = jnp.dot(amplitudes, aux_left, preferred_element_type=jnp.float32).astype(jnp.bfloat16)
    mixed = lax.dot_general(fitted, aux_right, (((1,), (1,)), ((), ())), preferred_element_type=jnp.float32)
    gap = virtual_energy[virtual_map] - occupied_energy[occupied_map]
    denominator = gap[:, None] + gap[None, :]
    return (mixed + mixed.T) / denominator
```

```python
import functools

import jax
import jax.numpy as jnp
from jax import lax
from jax.experimental import pallas as pl
from jax.experimental.pallas import tpu as pltpu
from jax.sharding import PartitionSpec as P

MESH = pl.DeviceIdType.MESH
SKEW = 2
HOP = 4
TILE = 128


def lookup(positions, energy_table):
    matches = positions[:, None] == jnp.arange(energy_table.shape[0], dtype=jnp.int32)[None, :]
    return jnp.sum(jnp.where(matches, energy_table[None, :], 0.0), axis=1)


def pair_gap(occupied_map, virtual_map, occupied_energy, virtual_energy, offset, length):
    occupied_part = lax.dynamic_slice_in_dim(occupied_map, offset, length, 0)
    virtual_part = lax.dynamic_slice_in_dim(virtual_map, offset, length, 0)
    return lookup(virtual_part, virtual_energy) - lookup(occupied_part, occupied_energy)


def gather_kernel(
    n_row, n_col, amp, left, right,
    fitted, mirror, right_cols, right_rows, line,
    amp_v, left_v, chain_v, pair_v, give_v, done_v,
    amp_sem, left_send, left_recv, rc_send, rc_recv,
    chain_send, chain_recv, pair_send, pair_recv,
    back_send, back_recv, done_sem, mir_send, mir_recv,
    line_send, line_recv, rr_send, rr_recv, half_send, half_recv,
    fit_send, fit_recv, own_sem,
):
    rows_here, cols_here = amp.shape
    fold = n_col // n_row
    folds = fold // 2
    n_z = n_col // 2
    tile = chain_v.shape[2]
    per_sub = cols_here // 2 // tile
    n_t = folds * per_sub
    n = n_row * n_t
    row = lax.axis_index("row")
    col = lax.axis_index("col")
    z = col // 2
    core = col % 2
    sib = {"col": col + 1 - 2 * core}
    owner = (col // fold) == row

    def remote(src, dst, send, recv, where):
        return pltpu.make_async_remote_copy(
            src_ref=src, dst_ref=dst, send_sem=send, recv_sem=recv,
            device_id=where, device_id_type=MESH,
        )

    def peer(b):
        return {"row": (row - b + n_row) % n_row}

    def start_row(m, d, t):
        return pl.multiple_of(
            (2 * (t // per_sub) + m) * cols_here + d * (cols_here // 2) + (t % per_sub) * tile, tile
        )

    barrier = pltpu.get_barrier_semaphore()
    pl.semaphore_signal(barrier, inc=1, device_id=sib, device_id_type=MESH)
    for b in range(1, n_row):
        pl.semaphore_signal(barrier, inc=1, device_id=peer(b), device_id_type=MESH)

    @pl.when(z > 0)
    def _():
        pl.semaphore_signal(barrier, inc=1, device_id={"col": col - 2}, device_id_type=MESH)

    @pl.when(z < n_z - 1)
    def _():
        pl.semaphore_signal(barrier, inc=1, device_id={"col": col + 2}, device_id_type=MESH)

    amp_copy = pltpu.make_async_copy(amp, amp_v, amp_sem)
    amp_copy.start()
    own_left = pltpu.make_async_copy(left, left_v.at[row], own_sem.at[0])
    own_left.start()
    own_rc = pltpu.make_async_copy(right, right_cols.at[row], own_sem.at[1])
    own_rc.start()
    own_line = pltpu.make_async_copy(right, line.at[z], own_sem.at[2])
    own_line.start()

    line_ends = (z + n_z - 1) // n_z + (2 * (n_z - 1) - z) // n_z
    pl.semaphore_wait(barrier, n_row + line_ends)

    def left_copy(b):
        return remote(left, left_v.at[row], left_send.at[b], left_recv.at[b], peer(b))

    def rc_copy(b):
        return remote(
            right, right_cols.at[row], rc_send.at[b], rc_recv.at[b], peer(b)
        )

    for b in range(1, n_row):
        left_copy(b).start()
    own_line.wait()
    own_left.wait()
    own_rc.wait()
    amp_copy.wait()

    def product(m, d, i):
        j = (row + i // n_t) % n_row
        rows = amp_v[pl.ds(start_row(m, d, i % n_t), tile), :]
        return jnp.dot(rows, left_v[j], preferred_element_type=jnp.float32)

    def place(d, i):
        j = (row + i // n_t) % n_row
        return (j, pl.ds(start_row(core, d, i % n_t), tile))

    def send_mirror(d, i, src):
        t = i % n_t
        j = (row + i // n_t) % n_row

        @pl.when(jnp.logical_and(owner, t // per_sub == (col % fold) // 2))
        def _():
            at = pl.multiple_of(d * (cols_here // 2) + (t % per_sub) * tile, tile)
            for b in range(1, n_row):
                remote(
                    src, mirror.at[j, pl.ds(at, tile)],
                    mir_send.at[b], mir_recv, peer(b),
                ).start()

    def back(d, i, src):
        block, rows = place(d, i)
        remote(
            src, fitted.at[block, rows], back_send.at[d], back_recv.at[d, i],
            {"col": col + (2 if d else -2)},
        ).start()

    def line_copy(way, h):
        block = z - h + 1 if way == 0 else z + h - 1
        return remote(
            line.at[block], line.at[block], line_send.at[way, h], line_recv.at[way, h],
            {"col": col + (2 if way == 0 else -2)},
        )

    def line_sends(way, h):
        if way == 0:
            return jnp.logical_and(z + 1 < n_z, z - h + 1 >= 0)
        return jnp.logical_and(z >= 1, z + h - 1 < n_z)

    def line_gets(way, h):
        return z - h >= 0 if way == 0 else z + h < n_z

    def spread_rows(block, _):
        block_col = 2 * block + core
        dest = block_col // fold
        at = pl.multiple_of((block_col % fold) * cols_here, cols_here)
        target = right_rows.at[row, pl.ds(at, cols_here)]
        part = (block_col % fold) // 2

        @pl.when(dest == row)
        def _():
            pltpu.make_async_copy(line.at[block], target, rr_send.at[block]).start()

        @pl.when(dest != row)
        def _():
            remote(
                line.at[block], target, rr_send.at[block], rr_recv.at[row * folds + part],
                {"row": dest},
            ).start()

        return 0

    def step(s, _):
        for b in range(1, n_row):

            @pl.when(s == b * n_t - 1)
            def _():
                left_copy(b).wait_recv()
                rc_copy(b).start()

        @pl.when(s % HOP == 0)
        def _():
            h = s // HOP

            @pl.when(jnp.logical_and(h >= 1, h < n_z))
            def _():
                for way in (0, 1):

                    @pl.when(line_gets(way, h))
                    def _():
                        line_copy(way, h).wait_recv()

            @pl.when(h + 1 < n_z)
            def _():
                for way in (0, 1):

                    @pl.when(line_sends(way, h + 1))
                    def _():
                        line_copy(way, h + 1).start()

            @pl.when(h == n_z)
            def _():
                lax.fori_loop(0, n_z, spread_rows, 0)

        for d in (0, 1):
            depth = z if d == 0 else n_z - 1 - z
            i = s - 1 - SKEW * depth

            @pl.when(jnp.logical_and(i + 1 >= 0, i + 1 < n))
            def _():
                k = i + 1
                give_v[d, k] = product(1 - core, d, k)
                remote(
                    give_v.at[d, k], pair_v.at[d, k], pair_send.at[d], pair_recv.at[d, k], sib
                ).start()

            @pl.when(jnp.logical_and(i >= 0, i < n))
            def _():
                mine = product(core, d, i)
                remote(
                    give_v.at[d, i], pair_v.at[d, i], pair_send.at[d], pair_recv.at[d, i], sib
                ).wait_recv()
                pair_v[d, i] = mine + pair_v[d, i]

                def onward():
                    return remote(
                        chain_v.at[d, i], chain_v.at[d, i], chain_send.at[d],
                        chain_recv.at[d, i], {"col": col + (-2 if d else 2)},
                    )

                @pl.when(depth == 0)
                def _():
                    chain_v[d, i] = pair_v[d, i]

                @pl.when(depth > 0)
                def _():
                    onward().wait_recv()
                    chain_v[d, i] = chain_v[d, i] + pair_v[d, i]

                @pl.when(depth < n_z - 1)
                def _():
                    onward().start()

                @pl.when(depth == n_z - 1)
                def _():
                    done_v[d, i] = chain_v[d, i].astype(done_v.dtype)
                    block, rows = place(d, i)
                    pltpu.make_async_copy(
                        done_v.at[d, i], fitted.at[block, rows], done_sem.at[d]
                    ).start()
                    back(d, i, done_v.at[d, i])
                    send_mirror(d, i, done_v.at[d, i])

            away = n_z - 1 - depth
            g = s - 1 - SKEW * (n_z - 1) - SKEW * away

            @pl.when(jnp.logical_and(away > 0, jnp.logical_and(g >= 0, g < n)))
            def _():
                block, rows = place(d, g)
                here = fitted.at[block, rows]
                remote(
                    here, here, back_send.at[d], back_recv.at[d, g], sib
                ).wait_recv()

                @pl.when(away < n_z - 1)
                def _():
                    back(d, g, here)

                send_mirror(d, g, here)

        return 0

    lax.fori_loop(0, n + 1 + 2 * SKEW * (n_z - 1), step, 0)

    def rr_wait(block, _):
        remote(
            line.at[block], line.at[block], rr_send.at[block], rr_recv.at[0], sib
        ).wait_send()
        return 0

    lax.fori_loop(0, n_z, rr_wait, 0)

    def rr_got(k, _):
        @pl.when(k // folds != row)
        def _():
            remote(line.at[0], line.at[0], rr_send.at[0], rr_recv.at[k], sib).wait_recv()

        return 0

    lax.fori_loop(0, n_row * folds, rr_got, 0)

    for d in (0, 1):
        depth = z if d == 0 else n_z - 1 - z

        @pl.when(depth == n_z - 1)
        def _():
            pltpu.make_async_copy(done_v.at[d], done_v.at[d], done_sem.at[d]).wait()

    def half(ref, u, send, recv):
        at = pl.multiple_of((2 * u + core) * cols_here, cols_here)
        part = ref.at[:, pl.ds(at, cols_here)]
        return remote(part, part, send.at[u], recv.at[u], sib)

    for u in range(folds):
        half(right_rows, u, half_send, half_recv).start()
        half(fitted, u, fit_send, fit_recv).start()

    @pl.when(owner)
    def _():
        at = pl.multiple_of((col % fold) * cols_here, cols_here)
        own = pltpu.make_async_copy(fitted.at[:, pl.ds(at, cols_here)], mirror, own_sem.at[3])
        own.start()
        for b in range(1, n_row):
            remote(mirror, mirror, mir_send.at[b], mir_recv, sib).wait_send()
        own.wait()

    @pl.when(jnp.logical_not(owner))
    def _():
        remote(mirror, mirror, mir_send.at[0], mir_recv, sib).wait_recv()

    for u in range(folds):
        half(right_rows, u, half_send, half_recv).wait()
        half(fitted, u, fit_send, fit_recv).wait()
    for b in range(1, n_row):
        left_copy(b).wait_send()
        rc_copy(b).wait()

    def line_wait(h, _):
        for way in (0, 1):

            @pl.when(line_sends(way, h))
            def _():
                line_copy(way, h).wait_send()

        return 0

    lax.fori_loop(1, n_z, line_wait, 0)
    for d in (0, 1):
        depth = z if d == 0 else n_z - 1 - z
        remote(
            give_v.at[d], pair_v.at[d], pair_send.at[d], pair_recv.at[d, 0], sib
        ).wait_send()

        @pl.when(depth < n_z - 1)
        def _():
            remote(
                chain_v.at[d], chain_v.at[d], chain_send.at[d], chain_recv.at[d, 0], sib
            ).wait_send()

        @pl.when(depth > 0)
        def _():
            remote(
                done_v.at[d], done_v.at[d], back_send.at[d], back_recv.at[d, 0], sib
            ).wait_send()


def gather_all(amplitudes, aux_left, aux_right):
    n_row, n_col = lax.axis_size("row"), lax.axis_size("col")
    rows_here, cols_here = amplitudes.shape
    aux_block = aux_left.shape[1]
    aux = aux_block * n_row
    folds = n_col // n_row // 2
    n_z = n_col // 2
    tile = min(TILE, cols_here // 2)
    n = n_row * (rows_here // 4 // tile)
    dma = pltpu.SemaphoreType.DMA
    anywhere = pl.BlockSpec(memory_space=pl.ANY)
    low = amplitudes.dtype
    shapes = [
        (n_row, rows_here, aux_block), (n_row, cols_here, aux_block),
        (n_row, cols_here, aux_block), (n_row, rows_here, aux_block),
        (n_z, cols_here, aux_block),
    ]
    return pl.pallas_call(
        functools.partial(gather_kernel, n_row, n_col),
        out_shape=[jax.ShapeDtypeStruct(s, low) for s in shapes],
        in_specs=[anywhere] * 3,
        out_specs=[anywhere] * 5,
        scratch_shapes=[
            pltpu.VMEM((rows_here, cols_here), low),
            pltpu.VMEM((n_row, cols_here, aux_block), low),
            pltpu.VMEM((2, n, tile, aux_block), jnp.float32),
            pltpu.VMEM((2, n, tile, aux_block), jnp.float32),
            pltpu.VMEM((2, n, tile, aux_block), jnp.float32),
            pltpu.VMEM((2, n, tile, aux_block), low),
            dma(()), dma((n_row,)), dma((n_row,)), dma((n_row,)), dma((n_row,)),
            dma((2,)), dma((2, n)), dma((2,)), dma((2, n)),
            dma((2,)), dma((2, n)), dma((2,)), dma((n_row,)), dma(()),
            dma((2, n_z)), dma((2, n_z)), dma((n_z,)), dma((n_row * folds,)),
            dma((folds,)), dma((folds,)), dma((folds,)), dma((folds,)), dma((4,)),
        ],
        compiler_params=pltpu.CompilerParams(
            collective_id=0, has_side_effects=True, vmem_limit_bytes=58 * 2**20
        ),
        cost_estimate=pl.CostEstimate(
            flops=2 * rows_here * cols_here * aux, bytes_accessed=2 * rows_here * cols_here,
            transcendentals=0,
        ),
        name="gather_all",
    )(amplitudes, aux_left, aux_right)


def finish_kernel(fitted, right_rows, right_cols, mirror, row_gap, col_gap, out, held):
    blocks = range(fitted.shape[0])

    @pl.when(pl.program_id(0) == 0)
    def _():
        held[...] = jnp.concatenate(
            [right_cols[j] for j in blocks] + [mirror[j] for j in blocks], axis=1
        )

    rows = jnp.concatenate([fitted[j] for j in blocks] + [right_rows[j] for j in blocks], axis=1)
    total = lax.dot_general(
        rows, held[...], (((1,), (1,)), ((), ())), preferred_element_type=jnp.float32
    )
    out[...] = total / (row_gap[...] + col_gap[...])


def finish(fitted, right_rows, right_cols, mirror, row_gap, col_gap):
    n_row, rows_here, aux_block = fitted.shape
    cols_here = mirror.shape[1]
    tile = min(256, rows_here)
    by_row = pl.BlockSpec((n_row, tile, aux_block), lambda i: (0, i, 0))
    whole = pl.BlockSpec((n_row, cols_here, aux_block), lambda i: (0, 0, 0))
    return pl.pallas_call(
        finish_kernel,
        grid=(rows_here // tile,),
        out_shape=jax.ShapeDtypeStruct((rows_here, cols_here), jnp.float32),
        in_specs=[
            by_row, by_row, whole, whole,
            pl.BlockSpec((tile, 1), lambda i: (i, 0)),
            pl.BlockSpec((1, cols_here), lambda i: (0, 0)),
        ],
        out_specs=pl.BlockSpec((tile, cols_here), lambda i: (i, 0)),
        scratch_shapes=[pltpu.VMEM((cols_here, 2 * n_row * aux_block), fitted.dtype)],
        compiler_params=pltpu.CompilerParams(vmem_limit_bytes=52 * 2**20),
        name="finish",
    )(fitted, right_rows, right_cols, mirror, row_gap, col_gap)


def per_device(
    amplitudes, aux_left, aux_right, occupied_map, virtual_map, occupied_energy, virtual_energy
):
    rows_here, cols_here = amplitudes.shape
    gap = functools.partial(pair_gap, occupied_map, virtual_map, occupied_energy, virtual_energy)
    row_gap = gap(lax.axis_index("row") * rows_here, rows_here)
    col_gap = gap(lax.axis_index("col") * cols_here, cols_here)
    fitted, mirror, right_cols, right_rows, _ = gather_all(amplitudes, aux_left, aux_right)
    return finish(
        fitted, right_rows, right_cols, mirror, row_gap[:, None], col_gap[None, :]
    )


def solution(mesh):
    return jax.shard_map(
        per_device,
        mesh=mesh,
        in_specs=(P("row", "col"), P("col", "row"), P("col", "row"), P(), P(), P(), P()),
        out_specs=P("row", "col"),
        check_vma=False,
    )
```

```python
import functools

import jax
import jax.numpy as jnp
from jax import lax
from jax.experimental import pallas as pl
from jax.experimental.pallas import tpu as pltpu
from jax.sharding import PartitionSpec as P

MESH = pl.DeviceIdType.MESH
SKEW = 2
HOP = 4
MIRROR_LAG = 1
RING_LAG = 4
TILE = 128


def lookup(positions, energy_table):
    matches = positions[:, None] == jnp.arange(energy_table.shape[0], dtype=jnp.int32)[None, :]
    return jnp.sum(jnp.where(matches, energy_table[None, :], 0.0), axis=1)


def pair_gap(occupied_map, virtual_map, occupied_energy, virtual_energy, offset, length):
    occupied_part = lax.dynamic_slice_in_dim(occupied_map, offset, length, 0)
    virtual_part = lax.dynamic_slice_in_dim(virtual_map, offset, length, 0)
    return lookup(virtual_part, virtual_energy) - lookup(occupied_part, occupied_energy)


def gather_kernel(
    n_row, n_col, amp, left, right,
    fitted, mirror, right_cols, right_rows, line,
    amp_v, left_v, chain_v, pair_v, give_v, done_v,
    amp_sem, left_send, left_recv, rc_send, rc_recv,
    chain_send, chain_recv, pair_send, pair_recv,
    back_send, back_recv, done_sem, mir_send, mir_recv,
    line_send, line_recv, rr_send, rr_recv, half_send, half_recv,
    fit_send, fit_recv, own_sem,
):
    rows_here, cols_here = amp.shape
    fold = n_col // n_row
    folds = fold // 2
    n_z = n_col // 2
    tile = chain_v.shape[2]
    per_sub = cols_here // 2 // tile
    n_t = folds * per_sub
    n = n_row * n_t
    row = lax.axis_index("row")
    col = lax.axis_index("col")
    z = col // 2
    core = col % 2
    sib = {"col": col + 1 - 2 * core}
    owner = (col // fold) == row

    def remote(src, dst, send, recv, where):
        return pltpu.make_async_remote_copy(
            src_ref=src, dst_ref=dst, send_sem=send, recv_sem=recv,
            device_id=where, device_id_type=MESH,
        )

    def peer(b):
        return {"row": (row - b + n_row) % n_row}

    def ring(p):
        turn = p // (n_row // 2)
        return (1 - turn) * p + turn * (n_row - 1 - p + n_row // 2)

    spot = ring(row)
    way_round = 1 - 2 * core
    next_row = {"row": ring((spot + way_round + n_row) % n_row)}
    owner_spot = ring(col // fold)
    hop = ((spot - owner_spot) * way_round + n_row) % n_row

    def behind(h):
        return ring((spot - h * way_round + h * n_row) % n_row)

    def aux_at(place, i):
        b = i // n_t
        moved = (b + n_row - 1) // n_row
        offset = moved * (n_row // 2 + (b // 2) * (2 * (b % 2) - 1))
        return ring((place + offset) % n_row)

    def start_row(m, d, t):
        return pl.multiple_of(
            (2 * (t // per_sub) + m) * cols_here + d * (cols_here // 2) + (t % per_sub) * tile, tile
        )

    barrier = pltpu.get_barrier_semaphore()
    pl.semaphore_signal(barrier, inc=1, device_id=sib, device_id_type=MESH)
    for b in range(1, n_row):
        pl.semaphore_signal(barrier, inc=1, device_id=peer(b), device_id_type=MESH)

    @pl.when(z > 0)
    def _():
        pl.semaphore_signal(barrier, inc=1, device_id={"col": col - 2}, device_id_type=MESH)

    @pl.when(z < n_z - 1)
    def _():
        pl.semaphore_signal(barrier, inc=1, device_id={"col": col + 2}, device_id_type=MESH)

    amp_copy = pltpu.make_async_copy(amp, amp_v, amp_sem)
    amp_copy.start()
    own_left = pltpu.make_async_copy(left, left_v.at[row], own_sem.at[0])
    own_left.start()
    own_rc = pltpu.make_async_copy(right, right_cols.at[row], own_sem.at[1])
    own_rc.start()
    own_line = pltpu.make_async_copy(right, line.at[z], own_sem.at[2])
    own_line.start()

    line_ends = (z + n_z - 1) // n_z + (2 * (n_z - 1) - z) // n_z
    pl.semaphore_wait(barrier, n_row + line_ends)

    def left_copy(h):
        block = left_v.at[behind(h - 1)]
        return remote(block, block, left_send.at[h], left_recv.at[h], next_row)

    def rc_copy(h):
        block = right_cols.at[behind(h - 1)]
        return remote(block, block, rc_send.at[h], rc_recv.at[h], next_row)

    own_left.wait()
    left_copy(1).start()
    own_line.wait()
    own_rc.wait()
    amp_copy.wait()

    def product(m, d, i):
        j = aux_at(spot, i)
        rows = amp_v[pl.ds(start_row(m, d, i % n_t), tile), :]
        return jnp.dot(rows, left_v[j], preferred_element_type=jnp.float32)

    def place(d, i):
        j = aux_at(spot, i)
        return (j, pl.ds(start_row(core, d, i % n_t), tile))

    def in_mirror(d, i):
        t = i % n_t
        at = pl.multiple_of(d * (cols_here // 2) + (t % per_sub) * tile, tile)
        return mirror.at[aux_at(owner_spot, i), pl.ds(at, tile)]

    def mirrored(i):
        return (i % n_t) // per_sub == (col % fold) // 2

    def send_mirror(d, i, src):
        remote(src, in_mirror(d, i), mir_send, mir_recv.at[d, i], next_row).start()

    def show(d, i, src):
        @pl.when(jnp.logical_and(owner, mirrored(i)))
        def _():
            send_mirror(d, i, src)

    def back(d, i, src):
        block, rows = place(d, i)
        remote(
            src, fitted.at[block, rows], back_send.at[d], back_recv.at[d, i],
            {"col": col + (2 if d else -2)},
        ).start()

    def line_copy(way, h):
        block = z - h + 1 if way == 0 else z + h - 1
        return remote(
            line.at[block], line.at[block], line_send.at[way, h], line_recv.at[way, h],
            {"col": col + (2 if way == 0 else -2)},
        )

    def line_sends(way, h):
        if way == 0:
            return jnp.logical_and(z + 1 < n_z, z - h + 1 >= 0)
        return jnp.logical_and(z >= 1, z + h - 1 < n_z)

    def line_gets(way, h):
        return z - h >= 0 if way == 0 else z + h < n_z

    def spread_rows(block, _):
        block_col = 2 * block + core
        dest = block_col // fold
        at = pl.multiple_of((block_col % fold) * cols_here, cols_here)
        target = right_rows.at[row, pl.ds(at, cols_here)]
        part = (block_col % fold) // 2

        @pl.when(dest == row)
        def _():
            pltpu.make_async_copy(line.at[block], target, rr_send.at[block]).start()

        @pl.when(dest != row)
        def _():
            remote(
                line.at[block], target, rr_send.at[block], rr_recv.at[row * folds + part],
                {"row": dest},
            ).start()

        return 0

    def step(s, _):
        half_way = n_row // 2
        for h in range(1, n_row):
            left_at = (n_t - 1) * h // half_way if h <= half_way else 2 * (h - half_way) * n_t - 1

            @pl.when(s == left_at)
            def _():
                left_copy(h).wait_recv()
                if h + 1 < n_row:
                    left_copy(h + 1).start()

            @pl.when(s == half_way * n_t + RING_LAG * (h - 1))
            def _():
                if h > 1:
                    rc_copy(h - 1).wait_recv()
                rc_copy(h).start()

        @pl.when(s % HOP == 0)
        def _():
            h = s // HOP

            @pl.when(jnp.logical_and(h >= 1, h < n_z))
            def _():
                for way in (0, 1):

                    @pl.when(line_gets(way, h))
                    def _():
                        line_copy(way, h).wait_recv()

            @pl.when(h + 1 < n_z)
            def _():
                for way in (0, 1):

                    @pl.when(line_sends(way, h + 1))
                    def _():
                        line_copy(way, h + 1).start()

            @pl.when(h == n_z)
            def _():
                lax.fori_loop(0, n_z, spread_rows, 0)

        for d in (0, 1):
            depth = z if d == 0 else n_z - 1 - z
            i = s - 1 - SKEW * depth

            @pl.when(jnp.logical_and(i + 1 >= 0, i + 1 < n))
            def _():
                k = i + 1
                give_v[d, k] = product(1 - core, d, k)
                remote(
                    give_v.at[d, k], pair_v.at[d, k], pair_send.at[d], pair_recv.at[d, k], sib
                ).start()

            @pl.when(jnp.logical_and(i >= 0, i < n))
            def _():
                mine = product(core, d, i)
                remote(
                    give_v.at[d, i], pair_v.at[d, i], pair_send.at[d], pair_recv.at[d, i], sib
                ).wait_recv()
                pair_v[d, i] = mine + pair_v[d, i]

                def onward():
                    return remote(
                        chain_v.at[d, i], chain_v.at[d, i], chain_send.at[d],
                        chain_recv.at[d, i], {"col": col + (-2 if d else 2)},
                    )

                @pl.when(depth == 0)
                def _():
                    chain_v[d, i] = pair_v[d, i]

                @pl.when(depth > 0)
                def _():
                    onward().wait_recv()
                    chain_v[d, i] = chain_v[d, i] + pair_v[d, i]

                @pl.when(depth < n_z - 1)
                def _():
                    onward().start()

                @pl.when(depth == n_z - 1)
                def _():
                    done_v[d, i] = chain_v[d, i].astype(done_v.dtype)
                    block, rows = place(d, i)
                    pltpu.make_async_copy(
                        done_v.at[d, i], fitted.at[block, rows], done_sem.at[d]
                    ).start()
                    back(d, i, done_v.at[d, i])
                    show(d, i, done_v.at[d, i])

            away = n_z - 1 - depth
            g = s - 1 - SKEW * (n_z - 1) - SKEW * away

            @pl.when(jnp.logical_and(away > 0, jnp.logical_and(g >= 0, g < n)))
            def _():
                block, rows = place(d, g)
                here = fitted.at[block, rows]
                remote(
                    here, here, back_send.at[d], back_recv.at[d, g], sib
                ).wait_recv()

                @pl.when(away < n_z - 1)
                def _():
                    back(d, g, here)

                show(d, g, here)

            x = g - MIRROR_LAG * hop

            @pl.when(
                jnp.logical_and(
                    jnp.logical_and(hop > 0, mirrored(x)), jnp.logical_and(x >= 0, x < n)
                )
            )
            def _():
                part = in_mirror(d, x)
                remote(part, part, mir_send, mir_recv.at[d, x], next_row).wait_recv()

                @pl.when(hop < n_row - 1)
                def _():
                    send_mirror(d, x, part)

        return 0

    steps = n + 1 + 2 * SKEW * (n_z - 1) + MIRROR_LAG * (n_row - 1)
    lax.fori_loop(0, steps, step, 0)

    def rr_wait(block, _):
        remote(
            line.at[block], line.at[block], rr_send.at[block], rr_recv.at[0], sib
        ).wait_send()
        return 0

    lax.fori_loop(0, n_z, rr_wait, 0)

    def rr_got(k, _):
        @pl.when(k // folds != row)
        def _():
            remote(line.at[0], line.at[0], rr_send.at[0], rr_recv.at[k], sib).wait_recv()

        return 0

    lax.fori_loop(0, n_row * folds, rr_got, 0)

    for d in (0, 1):
        depth = z if d == 0 else n_z - 1 - z

        @pl.when(depth == n_z - 1)
        def _():
            pltpu.make_async_copy(done_v.at[d], done_v.at[d], done_sem.at[d]).wait()

    def half(ref, u, send, recv):
        at = pl.multiple_of((2 * u + core) * cols_here, cols_here)
        part = ref.at[:, pl.ds(at, cols_here)]
        return remote(part, part, send.at[u], recv.at[u], sib)

    for u in range(folds):
        half(right_rows, u, half_send, half_recv).start()
        half(fitted, u, fit_send, fit_recv).start()

    @pl.when(owner)
    def _():
        at = pl.multiple_of((col % fold) * cols_here, cols_here)
        own = pltpu.make_async_copy(fitted.at[:, pl.ds(at, cols_here)], mirror, own_sem.at[3])
        own.start()
        own.wait()

    @pl.when(hop < n_row - 1)
    def _():
        remote(mirror, mirror, mir_send, mir_recv.at[0, 0], sib).wait_send()

    for u in range(folds):
        half(right_rows, u, half_send, half_recv).wait()
        half(fitted, u, fit_send, fit_recv).wait()
    rc_copy(n_row - 1).wait_recv()
    for h in range(1, n_row):
        left_copy(h).wait_send()
        rc_copy(h).wait_send()

    def line_wait(h, _):
        for way in (0, 1):

            @pl.when(line_sends(way, h))
            def _():
                line_copy(way, h).wait_send()

        return 0

    lax.fori_loop(1, n_z, line_wait, 0)
    for d in (0, 1):
        depth = z if d == 0 else n_z - 1 - z
        remote(
            give_v.at[d], pair_v.at[d], pair_send.at[d], pair_recv.at[d, 0], sib
        ).wait_send()

        @pl.when(depth < n_z - 1)
        def _():
            remote(
                chain_v.at[d], chain_v.at[d], chain_send.at[d], chain_recv.at[d, 0], sib
            ).wait_send()

        @pl.when(depth > 0)
        def _():
            remote(
                done_v.at[d], done_v.at[d], back_send.at[d], back_recv.at[d, 0], sib
            ).wait_send()


def gather_all(amplitudes, aux_left, aux_right):
    n_row, n_col = lax.axis_size("row"), lax.axis_size("col")
    rows_here, cols_here = amplitudes.shape
    aux_block = aux_left.shape[1]
    aux = aux_block * n_row
    folds = n_col // n_row // 2
    n_z = n_col // 2
    tile = min(TILE, cols_here // 2)
    n = n_row * (rows_here // 4 // tile)
    dma = pltpu.SemaphoreType.DMA
    anywhere = pl.BlockSpec(memory_space=pl.ANY)
    low = amplitudes.dtype
    shapes = [
        (n_row, rows_here, aux_block), (n_row, cols_here, aux_block),
        (n_row, cols_here, aux_block), (n_row, rows_here, aux_block),
        (n_z, cols_here, aux_block),
    ]
    return pl.pallas_call(
        functools.partial(gather_kernel, n_row, n_col),
        out_shape=[jax.ShapeDtypeStruct(s, low) for s in shapes],
        in_specs=[anywhere] * 3,
        out_specs=[anywhere] * 5,
        scratch_shapes=[
            pltpu.VMEM((rows_here, cols_here), low),
            pltpu.VMEM((n_row, cols_here, aux_block), low),
            pltpu.VMEM((2, n, tile, aux_block), jnp.float32),
            pltpu.VMEM((2, n, tile, aux_block), jnp.float32),
            pltpu.VMEM((2, n, tile, aux_block), jnp.float32),
            pltpu.VMEM((2, n, tile, aux_block), low),
            dma(()), dma((n_row,)), dma((n_row,)), dma((n_row,)), dma((n_row,)),
            dma((2,)), dma((2, n)), dma((2,)), dma((2, n)),
            dma((2,)), dma((2, n)), dma((2,)), dma(()), dma((2, n)),
            dma((2, n_z)), dma((2, n_z)), dma((n_z,)), dma((n_row * folds,)),
            dma((folds,)), dma((folds,)), dma((folds,)), dma((folds,)), dma((4,)),
        ],
        compiler_params=pltpu.CompilerParams(
            collective_id=0, has_side_effects=True, vmem_limit_bytes=58 * 2**20
        ),
        cost_estimate=pl.CostEstimate(
            flops=2 * rows_here * cols_here * aux, bytes_accessed=2 * rows_here * cols_here,
            transcendentals=0,
        ),
        name="gather_all",
    )(amplitudes, aux_left, aux_right)


def finish_kernel(fitted, right_rows, right_cols, mirror, row_gap, col_gap, out, held):
    blocks = range(fitted.shape[0])

    @pl.when(pl.program_id(0) == 0)
    def _():
        held[...] = jnp.concatenate(
            [right_cols[j] for j in blocks] + [mirror[j] for j in blocks], axis=1
        )

    rows = jnp.concatenate([fitted[j] for j in blocks] + [right_rows[j] for j in blocks], axis=1)
    total = lax.dot_general(
        rows, held[...], (((1,), (1,)), ((), ())), preferred_element_type=jnp.float32
    )
    out[...] = total / (row_gap[...] + col_gap[...])


def finish(fitted, right_rows, right_cols, mirror, row_gap, col_gap):
    n_row, rows_here, aux_block = fitted.shape
    cols_here = mirror.shape[1]
    tile = min(256, rows_here)
    by_row = pl.BlockSpec((n_row, tile, aux_block), lambda i: (0, i, 0))
    whole = pl.BlockSpec((n_row, cols_here, aux_block), lambda i: (0, 0, 0))
    return pl.pallas_call(
        finish_kernel,
        grid=(rows_here // tile,),
        out_shape=jax.ShapeDtypeStruct((rows_here, cols_here), jnp.float32),
        in_specs=[
            by_row, by_row, whole, whole,
            pl.BlockSpec((tile, 1), lambda i: (i, 0)),
            pl.BlockSpec((1, cols_here), lambda i: (0, 0)),
        ],
        out_specs=pl.BlockSpec((tile, cols_here), lambda i: (i, 0)),
        scratch_shapes=[pltpu.VMEM((cols_here, 2 * n_row * aux_block), fitted.dtype)],
        compiler_params=pltpu.CompilerParams(vmem_limit_bytes=52 * 2**20),
        name="finish",
    )(fitted, right_rows, right_cols, mirror, row_gap, col_gap)


def per_device(
    amplitudes, aux_left, aux_right, occupied_map, virtual_map, occupied_energy, virtual_energy
):
    rows_here, cols_here = amplitudes.shape
    gap = functools.partial(pair_gap, occupied_map, virtual_map, occupied_energy, virtual_energy)
    row_gap = gap(lax.axis_index("row") * rows_here, rows_here)
    col_gap = gap(lax.axis_index("col") * cols_here, cols_here)
    fitted, mirror, right_cols, right_rows, _ = gather_all(amplitudes, aux_left, aux_right)
    return finish(
        fitted, right_rows, right_cols, mirror, row_gap[:, None], col_gap[None, :]
    )


def solution(mesh):
    return jax.shard_map(
        per_device,
        mesh=mesh,
        in_specs=(P("row", "col"), P("col", "row"), P("col", "row"), P(), P(), P(), P()),
        out_specs=P("row", "col"),
        check_vma=False,
    )
```

```python
import functools

import jax
import jax.numpy as jnp
from jax import lax
from jax.experimental import pallas as pl
from jax.experimental.pallas import tpu as pltpu
from jax.sharding import PartitionSpec as P

MESH = pl.DeviceIdType.MESH
SKEW = 2
HOP = 4
MIRROR_LAG = 1
RING_LAG = 4
SLOTS = 8
TILE = 128


def lookup(positions, energy_table):
    matches = positions[:, None] == jnp.arange(energy_table.shape[0], dtype=jnp.int32)[None, :]
    return jnp.sum(jnp.where(matches, energy_table[None, :], 0.0), axis=1)


def pair_gap(occupied_map, virtual_map, occupied_energy, virtual_energy, offset, length):
    occupied_part = lax.dynamic_slice_in_dim(occupied_map, offset, length, 0)
    virtual_part = lax.dynamic_slice_in_dim(virtual_map, offset, length, 0)
    return lookup(virtual_part, virtual_energy) - lookup(occupied_part, occupied_energy)


def gather_kernel(
    n_row, n_col, amp, left, right,
    fitted, mirror, right_cols, right_rows,
    amp_v, left_v, chain_v, pair_v, give_v, done_v, line_v, rr_v, mir_v,
    amp_sem, own_sem, left_send, left_recv, rc_send, rc_recv,
    chain_send, chain_recv, pair_send, pair_recv,
    back_send, back_recv, done_sem, fit_send, fit_recv,
    mir_send, mir_recv, mir_own,
    line_send, line_recv, rr_send, rr_recv, rr_own, half_send, half_recv,
):
    rows_here, cols_here = amp.shape
    fold = n_col // n_row
    folds = fold // 2
    n_z = n_col // 2
    tile = chain_v.shape[2]
    per_sub = cols_here // 2 // tile
    n_t = folds * per_sub
    n = n_row * n_t
    row = lax.axis_index("row")
    col = lax.axis_index("col")
    z = col // 2
    core = col % 2
    sib = {"col": col + 1 - 2 * core}
    owner = (col // fold) == row

    def remote(src, dst, send, recv, where):
        return pltpu.make_async_remote_copy(
            src_ref=src, dst_ref=dst, send_sem=send, recv_sem=recv,
            device_id=where, device_id_type=MESH,
        )

    def peer(b):
        return {"row": (row - b + n_row) % n_row}

    def ring(p):
        turn = p // (n_row // 2)
        return (1 - turn) * p + turn * (n_row - 1 - p + n_row // 2)

    spot = ring(row)
    way_round = 1 - 2 * core
    next_row = {"row": ring((spot + way_round + n_row) % n_row)}
    owner_spot = ring(col // fold)
    hop = ((spot - owner_spot) * way_round + n_row) % n_row

    def behind(h):
        return ring((spot - h * way_round + h * n_row) % n_row)

    def aux_at(place, i):
        b = i // n_t
        moved = (b + n_row - 1) // n_row
        offset = moved * (n_row // 2 + (b // 2) * (2 * (b % 2) - 1))
        return ring((place + offset) % n_row)

    def start_row(m, d, t):
        return pl.multiple_of(
            (2 * (t // per_sub) + m) * cols_here + d * (cols_here // 2) + (t % per_sub) * tile, tile
        )

    barrier = pltpu.get_barrier_semaphore()
    pl.semaphore_signal(barrier, inc=1, device_id=sib, device_id_type=MESH)
    for b in range(1, n_row):
        pl.semaphore_signal(barrier, inc=1, device_id=peer(b), device_id_type=MESH)

    @pl.when(z > 0)
    def _():
        pl.semaphore_signal(barrier, inc=1, device_id={"col": col - 2}, device_id_type=MESH)

    @pl.when(z < n_z - 1)
    def _():
        pl.semaphore_signal(barrier, inc=1, device_id={"col": col + 2}, device_id_type=MESH)

    amp_copy = pltpu.make_async_copy(amp, amp_v, amp_sem)
    amp_copy.start()
    own_left = pltpu.make_async_copy(left, left_v.at[row], own_sem.at[0])
    own_left.start()
    own_line = pltpu.make_async_copy(right, line_v.at[z], own_sem.at[1])
    own_line.start()

    line_ends = (z + n_z - 1) // n_z + (2 * (n_z - 1) - z) // n_z
    pl.semaphore_wait(barrier, n_row + line_ends)

    def left_copy(h):
        block = left_v.at[behind(h - 1)]
        return remote(block, block, left_send.at[h], left_recv.at[h], next_row)

    def rc_copy(b):
        return remote(
            line_v.at[z], right_cols.at[row], rc_send.at[b], rc_recv.at[b], peer(b)
        )

    own_left.wait()
    left_copy(1).start()
    own_line.wait()
    own_rc = pltpu.make_async_copy(line_v.at[z], right_cols.at[row], own_sem.at[2])
    own_rc.start()
    amp_copy.wait()

    def product(m, d, i):
        j = aux_at(spot, i)
        rows = amp_v[pl.ds(start_row(m, d, i % n_t), tile), :]
        return jnp.dot(rows, left_v[j], preferred_element_type=jnp.float32)

    def place(d, i):
        j = aux_at(spot, i)
        return (j, pl.ds(start_row(core, d, i % n_t), tile))

    def mirrored(i):
        return (i % n_t) // per_sub == (col % fold) // 2

    def mirror_copy(d, i, src):
        t = i % n_t
        at = pl.multiple_of(d * (cols_here // 2) + (t % per_sub) * tile, tile)
        target = mirror.at[aux_at(owner_spot, i), pl.ds(at, tile)]
        pltpu.make_async_copy(src, target, mir_own).start()

        @pl.when(hop < n_row - 1)
        def _():
            remote(src, mir_v.at[d, i], mir_send, mir_recv.at[d, i], next_row).start()

    def arrived(d, i):
        chunk = done_v.at[d, i]
        block, rows = place(d, i)
        target = fitted.at[block, rows]
        remote(chunk, target, fit_send.at[d], fit_recv.at[d], sib).start()
        pltpu.make_async_copy(chunk, target, done_sem.at[d]).start()

        @pl.when(jnp.logical_and(owner, mirrored(i)))
        def _():
            mirror_copy(d, i, chunk)

    def back(d, i):
        chunk = done_v.at[d, i]
        return remote(
            chunk, chunk, back_send.at[d], back_recv.at[d, i], {"col": col + (2 if d else -2)}
        )

    def line_copy(way, h):
        block = z - h + 1 if way == 0 else z + h - 1
        return remote(
            line_v.at[block], line_v.at[block], line_send.at[way, h], line_recv.at[way, h],
            {"col": col + (2 if way == 0 else -2)},
        )

    def line_sends(way, h):
        if way == 0:
            return jnp.logical_and(z + 1 < n_z, z - h + 1 >= 0)
        return jnp.logical_and(z >= 1, z + h - 1 < n_z)

    def line_gets(way, h):
        return z - h >= 0 if way == 0 else z + h < n_z

    def rows_of(block):
        block_col = 2 * block + core
        dest = block_col // fold
        part = (block_col % fold) // 2
        return dest, remote(
            line_v.at[block], rr_v.at[row, part], rr_send.at[block],
            rr_recv.at[row * folds + part], {"row": dest},
        )

    def spread_rows(block, _):
        dest, copy = rows_of(block)

        @pl.when(dest != row)
        def _():
            copy.start()

        return 0

    def spread_wait(block, _):
        dest, copy = rows_of(block)

        @pl.when(dest != row)
        def _():
            copy.wait_send()

        return 0

    def keep_rows(k, _):
        source = k // folds
        part = k % folds
        at = pl.multiple_of((2 * part + core) * cols_here, cols_here)
        target = right_rows.at[source, pl.ds(at, cols_here)]

        def keep(src):
            pltpu.make_async_copy(src, target, rr_own).start()
            remote(src, target, half_send, half_recv, sib).start()

        @pl.when(source == row)
        def _():
            keep(line_v.at[row * folds + part])

        @pl.when(source != row)
        def _():
            here = rr_v.at[source, part]
            remote(here, here, rr_send.at[0], rr_recv.at[k], sib).wait_recv()
            keep(here)

        return 0

    def give(d, k):
        return remote(
            give_v.at[d, k % SLOTS], pair_v.at[d, k], pair_send.at[d, k % SLOTS],
            pair_recv.at[d, k], sib,
        )

    def step(s, _):
        half_way = n_row // 2
        for h in range(1, n_row):
            left_at = (n_t - 1) * h // half_way if h <= half_way else 2 * (h - half_way) * n_t - 1

            @pl.when(s == left_at)
            def _():
                left_copy(h).wait_recv()
                if h + 1 < n_row:
                    left_copy(h + 1).start()

            @pl.when(s == half_way * n_t + RING_LAG * (h - 1))
            def _():
                rc_copy(h).start()

        @pl.when(s % HOP == 0)
        def _():
            h = s // HOP

            @pl.when(jnp.logical_and(h >= 1, h < n_z))
            def _():
                for way in (0, 1):

                    @pl.when(line_gets(way, h))
                    def _():
                        line_copy(way, h).wait_recv()

            @pl.when(h + 1 < n_z)
            def _():
                for way in (0, 1):

                    @pl.when(line_sends(way, h + 1))
                    def _():
                        line_copy(way, h + 1).start()

            @pl.when(h == n_z)
            def _():
                lax.fori_loop(0, n_z, spread_rows, 0)

            @pl.when(h == n_z + 3)
            def _():
                lax.fori_loop(0, n_row * folds, keep_rows, 0)

        for d in (0, 1):
            depth = z if d == 0 else n_z - 1 - z
            i = s - 1 - SKEW * depth

            @pl.when(jnp.logical_and(i + 1 >= 0, i + 1 < n))
            def _():
                k = i + 1

                @pl.when(k >= SLOTS)
                def _():
                    give(d, k).wait_send()

                give_v[d, k % SLOTS] = product(1 - core, d, k)
                give(d, k).start()

            @pl.when(jnp.logical_and(i >= 0, i < n))
            def _():
                mine = product(core, d, i)
                give(d, i).wait_recv()
                pair_v[d, i] = mine + pair_v[d, i]

                def onward():
                    return remote(
                        chain_v.at[d, i], chain_v.at[d, i], chain_send.at[d],
                        chain_recv.at[d, i], {"col": col + (-2 if d else 2)},
                    )

                @pl.when(depth == 0)
                def _():
                    chain_v[d, i] = pair_v[d, i]

                @pl.when(depth > 0)
                def _():
                    onward().wait_recv()
                    chain_v[d, i] = chain_v[d, i] + pair_v[d, i]

                @pl.when(depth < n_z - 1)
                def _():
                    onward().start()

                @pl.when(depth == n_z - 1)
                def _():
                    done_v[d, i] = chain_v[d, i].astype(done_v.dtype)
                    back(d, i).start()
                    arrived(d, i)

            away = n_z - 1 - depth
            g = s - 1 - SKEW * (n_z - 1) - SKEW * away

            @pl.when(jnp.logical_and(away > 0, jnp.logical_and(g >= 0, g < n)))
            def _():
                back(d, g).wait_recv()

                @pl.when(away < n_z - 1)
                def _():
                    back(d, g).start()

                arrived(d, g)

            x = g - MIRROR_LAG * hop

            @pl.when(
                jnp.logical_and(
                    jnp.logical_and(hop > 0, mirrored(x)), jnp.logical_and(x >= 0, x < n)
                )
            )
            def _():
                part = mir_v.at[d, x]
                remote(part, part, mir_send, mir_recv.at[d, x], next_row).wait_recv()
                mirror_copy(d, x, part)

        return 0

    steps = n + 1 + 2 * SKEW * (n_z - 1) + MIRROR_LAG * (n_row - 1)
    lax.fori_loop(0, steps, step, 0)

    lax.fori_loop(0, n_z, spread_wait, 0)
    pltpu.make_async_copy(rr_v, rr_v, rr_own).wait()
    remote(rr_v, rr_v, half_send, half_recv, sib).wait()
    pltpu.make_async_copy(mirror, mirror, mir_own).wait()

    @pl.when(hop < n_row - 1)
    def _():
        remote(mirror, mirror, mir_send, mir_recv.at[0, 0], sib).wait_send()

    own_rc.wait()
    for h in range(1, n_row):
        left_copy(h).wait_send()
        rc_copy(h).wait()

    def line_wait(h, _):
        for way in (0, 1):

            @pl.when(line_sends(way, h))
            def _():
                line_copy(way, h).wait_send()

        return 0

    lax.fori_loop(1, n_z, line_wait, 0)
    for d in (0, 1):
        depth = z if d == 0 else n_z - 1 - z
        pltpu.make_async_copy(done_v.at[d], done_v.at[d], done_sem.at[d]).wait()
        remote(done_v.at[d], done_v.at[d], fit_send.at[d], fit_recv.at[d], sib).wait()
        for k in range(n - SLOTS, n):
            give(d, k).wait_send()

        @pl.when(depth < n_z - 1)
        def _():
            remote(
                chain_v.at[d], chain_v.at[d], chain_send.at[d], chain_recv.at[d, 0], sib
            ).wait_send()

        @pl.when(depth > 0)
        def _():
            remote(
                done_v.at[d], done_v.at[d], back_send.at[d], back_recv.at[d, 0], sib
            ).wait_send()


def gather_all(amplitudes, aux_left, aux_right):
    n_row, n_col = lax.axis_size("row"), lax.axis_size("col")
    rows_here, cols_here = amplitudes.shape
    aux_block = aux_left.shape[1]
    aux = aux_block * n_row
    folds = n_col // n_row // 2
    n_z = n_col // 2
    tile = min(TILE, cols_here // 2)
    n = n_row * (rows_here // 4 // tile)
    dma = pltpu.SemaphoreType.DMA
    anywhere = pl.BlockSpec(memory_space=pl.ANY)
    low = amplitudes.dtype
    shapes = [
        (n_row, rows_here, aux_block), (n_row, cols_here, aux_block),
        (n_row, cols_here, aux_block), (n_row, rows_here, aux_block),
    ]
    return pl.pallas_call(
        functools.partial(gather_kernel, n_row, n_col),
        out_shape=[jax.ShapeDtypeStruct(s, low) for s in shapes],
        in_specs=[anywhere] * 3,
        out_specs=[anywhere] * 4,
        scratch_shapes=[
            pltpu.VMEM((rows_here, cols_here), low),
            pltpu.VMEM((n_row, cols_here, aux_block), low),
            pltpu.VMEM((2, n, tile, aux_block), jnp.float32),
            pltpu.VMEM((2, n, tile, aux_block), jnp.float32),
            pltpu.VMEM((2, SLOTS, tile, aux_block), jnp.float32),
            pltpu.VMEM((2, n, tile, aux_block), low),
            pltpu.VMEM((n_z, cols_here, aux_block), low),
            pltpu.VMEM((n_row, folds, cols_here, aux_block), low),
            pltpu.VMEM((2, n, tile, aux_block), low),
            dma(()), dma((3,)), dma((n_row,)), dma((n_row,)), dma((n_row,)), dma((n_row,)),
            dma((2,)), dma((2, n)), dma((2, SLOTS)), dma((2, n)),
            dma((2,)), dma((2, n)), dma((2,)), dma((2,)), dma((2,)),
            dma(()), dma((2, n)), dma(()),
            dma((2, n_z)), dma((2, n_z)), dma((n_z,)), dma((n_row * folds,)),
            dma(()), dma(()), dma(()),
        ],
        compiler_params=pltpu.CompilerParams(
            collective_id=0, has_side_effects=True, vmem_limit_bytes=60 * 2**20
        ),
        cost_estimate=pl.CostEstimate(
            flops=2 * rows_here * cols_here * aux, bytes_accessed=2 * rows_here * cols_here,
            transcendentals=0,
        ),
        name="gather_all",
    )(amplitudes, aux_left, aux_right)


def finish_kernel(fitted, right_rows, right_cols, mirror, row_gap, col_gap, out, held):
    blocks = range(fitted.shape[0])

    @pl.when(pl.program_id(0) == 0)
    def _():
        held[...] = jnp.concatenate(
            [right_cols[j] for j in blocks] + [mirror[j] for j in blocks], axis=1
        )

    rows = jnp.concatenate([fitted[j] for j in blocks] + [right_rows[j] for j in blocks], axis=1)
    total = lax.dot_general(
        rows, held[...], (((1,), (1,)), ((), ())), preferred_element_type=jnp.float32
    )
    out[...] = total / (row_gap[...] + col_gap[...])


def finish(fitted, right_rows, right_cols, mirror, row_gap, col_gap):
    n_row, rows_here, aux_block = fitted.shape
    cols_here = mirror.shape[1]
    tile = min(256, rows_here)
    by_row = pl.BlockSpec((n_row, tile, aux_block), lambda i: (0, i, 0))
    whole = pl.BlockSpec((n_row, cols_here, aux_block), lambda i: (0, 0, 0))
    return pl.pallas_call(
        finish_kernel,
        grid=(rows_here // tile,),
        out_shape=jax.ShapeDtypeStruct((rows_here, cols_here), jnp.float32),
        in_specs=[
            by_row, by_row, whole, whole,
            pl.BlockSpec((tile, 1), lambda i: (i, 0)),
            pl.BlockSpec((1, cols_here), lambda i: (0, 0)),
        ],
        out_specs=pl.BlockSpec((tile, cols_here), lambda i: (i, 0)),
        scratch_shapes=[pltpu.VMEM((cols_here, 2 * n_row * aux_block), fitted.dtype)],
        compiler_params=pltpu.CompilerParams(vmem_limit_bytes=52 * 2**20),
        name="finish",
    )(fitted, right_rows, right_cols, mirror, row_gap, col_gap)


def per_device(
    amplitudes, aux_left, aux_right, occupied_map, virtual_map, occupied_energy, virtual_energy
):
    rows_here, cols_here = amplitudes.shape
    gap = functools.partial(pair_gap, occupied_map, virtual_map, occupied_energy, virtual_energy)
    row_gap = gap(lax.axis_index("row") * rows_here, rows_here)
    col_gap = gap(lax.axis_index("col") * cols_here, cols_here)
    fitted, mirror, right_cols, right_rows = gather_all(amplitudes, aux_left, aux_right)
    return finish(
        fitted, right_rows, right_cols, mirror, row_gap[:, None], col_gap[None, :]
    )


def solution(mesh):
    return jax.shard_map(
        per_device,
        mesh=mesh,
        in_specs=(P("row", "col"), P("col", "row"), P("col", "row"), P(), P(), P(), P()),
        out_specs=P("row", "col"),
        check_vma=False,
    )
```

```python
import functools

import jax
import jax.numpy as jnp
from jax import lax
from jax.experimental import pallas as pl
from jax.experimental.pallas import tpu as pltpu
from jax.sharding import PartitionSpec as P

MESH = pl.DeviceIdType.MESH
SKEW = 3
HOP = 8
MIRROR_LAG = 6
RING_LAG = 8
SLOTS = 8
TILE = 128


def lookup(positions, energy_table):
    matches = positions[:, None] == jnp.arange(energy_table.shape[0], dtype=jnp.int32)[None, :]
    return jnp.sum(jnp.where(matches, energy_table[None, :], 0.0), axis=1)


def pair_gap(occupied_map, virtual_map, occupied_energy, virtual_energy, offset, length):
    occupied_part = lax.dynamic_slice_in_dim(occupied_map, offset, length, 0)
    virtual_part = lax.dynamic_slice_in_dim(virtual_map, offset, length, 0)
    return lookup(virtual_part, virtual_energy) - lookup(occupied_part, occupied_energy)


def gather_kernel(
    n_row, n_col, amp, left, right,
    fitted, mirror, right_cols, right_rows,
    amp_v, left_v, chain_v, pair_v, give_v, done_v, line_v, rr_v, mir_v,
    amp_sem, own_sem, left_send, left_recv, rc_send, rc_recv,
    chain_send, chain_recv, pair_send, pair_recv,
    back_send, back_recv, done_sem, fit_send, fit_recv,
    mir_send, mir_recv, mir_own,
    line_send, line_recv, rr_send, rr_recv, rr_own, half_send, half_recv,
):
    rows_here, cols_here = amp.shape
    fold = n_col // n_row
    folds = fold // 2
    n_z = n_col // 2
    tile = chain_v.shape[2]
    per_sub = cols_here // 2 // tile
    n_t = folds * per_sub
    n = n_row * n_t
    row = lax.axis_index("row")
    col = lax.axis_index("col")
    z = col // 2
    core = col % 2
    sib = {"col": col + 1 - 2 * core}
    owner = (col // fold) == row

    def remote(src, dst, send, recv, where):
        return pltpu.make_async_remote_copy(
            src_ref=src, dst_ref=dst, send_sem=send, recv_sem=recv,
            device_id=where, device_id_type=MESH,
        )

    def peer(b):
        return {"row": (row - b + n_row) % n_row}

    def ring(p):
        turn = p // (n_row // 2)
        return (1 - turn) * p + turn * (n_row - 1 - p + n_row // 2)

    spot = ring(row)
    way_round = 1 - 2 * core
    next_row = {"row": ring((spot + way_round + n_row) % n_row)}
    owner_spot = ring(col // fold)
    hop = ((spot - owner_spot) * way_round + n_row) % n_row

    def behind(h):
        return ring((spot - h * way_round + h * n_row) % n_row)

    def aux_at(place, i):
        b = i // n_t
        moved = (b + n_row - 1) // n_row
        offset = moved * (n_row // 2 + (b // 2) * (2 * (b % 2) - 1))
        return ring((place + offset) % n_row)

    def start_row(m, d, t):
        return pl.multiple_of(
            (2 * (t // per_sub) + m) * cols_here + d * (cols_here // 2) + (t % per_sub) * tile, tile
        )

    barrier = pltpu.get_barrier_semaphore()
    pl.semaphore_signal(barrier, inc=1, device_id=sib, device_id_type=MESH)
    for b in range(1, n_row):
        pl.semaphore_signal(barrier, inc=1, device_id=peer(b), device_id_type=MESH)

    @pl.when(z > 0)
    def _():
        pl.semaphore_signal(barrier, inc=1, device_id={"col": col - 2}, device_id_type=MESH)

    @pl.when(z < n_z - 1)
    def _():
        pl.semaphore_signal(barrier, inc=1, device_id={"col": col + 2}, device_id_type=MESH)

    amp_copy = pltpu.make_async_copy(amp, amp_v, amp_sem)
    amp_copy.start()
    own_left = pltpu.make_async_copy(left, left_v.at[row], own_sem.at[0])
    own_left.start()
    own_line = pltpu.make_async_copy(right, line_v.at[z], own_sem.at[1])
    own_line.start()

    line_ends = (z + n_z - 1) // n_z + (2 * (n_z - 1) - z) // n_z
    pl.semaphore_wait(barrier, n_row + line_ends)

    def left_copy(h):
        block = left_v.at[behind(h - 1)]
        return remote(block, block, left_send.at[h], left_recv.at[h], next_row)

    def rc_copy(b):
        return remote(
            line_v.at[z], right_cols.at[row], rc_send.at[b], rc_recv.at[b], peer(b)
        )

    own_left.wait()
    left_copy(1).start()
    own_line.wait()
    own_rc = pltpu.make_async_copy(line_v.at[z], right_cols.at[row], own_sem.at[2])
    own_rc.start()
    amp_copy.wait()

    def product(m, d, i):
        j = aux_at(spot, i)
        rows = amp_v[pl.ds(start_row(m, d, i % n_t), tile), :]
        return jnp.dot(rows, left_v[j], preferred_element_type=jnp.float32)

    def place(d, i):
        j = aux_at(spot, i)
        return (j, pl.ds(start_row(core, d, i % n_t), tile))

    def mirrored(i):
        return (i % n_t) // per_sub == (col % fold) // 2

    def mirror_copy(d, i, src):
        t = i % n_t
        at = pl.multiple_of(d * (cols_here // 2) + (t % per_sub) * tile, tile)
        target = mirror.at[aux_at(owner_spot, i), pl.ds(at, tile)]
        pltpu.make_async_copy(src, target, mir_own).start()

        @pl.when(hop < n_row - 1)
        def _():
            remote(src, mir_v.at[d, i], mir_send, mir_recv.at[d, i], next_row).start()

    def arrived(d, i):
        chunk = done_v.at[d, i]
        block, rows = place(d, i)
        target = fitted.at[block, rows]
        remote(chunk, target, fit_send.at[d], fit_recv.at[d], sib).start()
        pltpu.make_async_copy(chunk, target, done_sem.at[d]).start()

        @pl.when(jnp.logical_and(owner, mirrored(i)))
        def _():
            mirror_copy(d, i, chunk)

    def back(d, i):
        chunk = done_v.at[d, i]
        return remote(
            chunk, chunk, back_send.at[d], back_recv.at[d, i], {"col": col + (2 if d else -2)}
        )

    def line_copy(way, h):
        block = z - h + 1 if way == 0 else z + h - 1
        return remote(
            line_v.at[block], line_v.at[block], line_send.at[way, h], line_recv.at[way, h],
            {"col": col + (2 if way == 0 else -2)},
        )

    def line_sends(way, h):
        if way == 0:
            return jnp.logical_and(z + 1 < n_z, z - h + 1 >= 0)
        return jnp.logical_and(z >= 1, z + h - 1 < n_z)

    def line_gets(way, h):
        return z - h >= 0 if way == 0 else z + h < n_z

    def rows_of(block):
        block_col = 2 * block + core
        dest = block_col // fold
        part = (block_col % fold) // 2
        return dest, remote(
            line_v.at[block], rr_v.at[row, part], rr_send.at[block],
            rr_recv.at[row * folds + part], {"row": dest},
        )

    def spread_rows(block):
        dest, copy = rows_of(block)

        @pl.when(dest != row)
        def _():
            copy.start()

    def spread_wait(block, _):
        dest, copy = rows_of(block)

        @pl.when(dest != row)
        def _():
            copy.wait_send()

        return 0

    def keep_rows(k, _):
        source = k // folds
        part = k % folds
        at = pl.multiple_of((2 * part + core) * cols_here, cols_here)
        target = right_rows.at[source, pl.ds(at, cols_here)]

        def keep(src):
            pltpu.make_async_copy(src, target, rr_own).start()
            remote(src, target, half_send, half_recv, sib).start()

        @pl.when(source == row)
        def _():
            keep(line_v.at[row * folds + part])

        @pl.when(source != row)
        def _():
            here = rr_v.at[source, part]
            remote(here, here, rr_send.at[0], rr_recv.at[k], sib).wait_recv()
            keep(here)

        return 0

    def give(d, k):
        return remote(
            give_v.at[d, k % SLOTS], pair_v.at[d, k], pair_send.at[d, k % SLOTS],
            pair_recv.at[d, k], sib,
        )

    def step(s, _):
        half_way = n_row // 2
        for h in range(1, n_row):
            left_at = (n_t - 1) * h // half_way if h <= half_way else 2 * (h - half_way) * n_t - 1

            @pl.when(s == left_at)
            def _():
                left_copy(h).wait_recv()
                if h + 1 < n_row:
                    left_copy(h + 1).start()

            @pl.when(s == half_way * n_t + RING_LAG * (h - 2) + 2)
            def _():
                rc_copy(h).start()

        @pl.when(s % HOP == 0)
        def _():
            h = s // HOP

            @pl.when(jnp.logical_and(h >= 1, h < n_z))
            def _():
                for way in (0, 1):

                    @pl.when(line_gets(way, h))
                    def _():
                        line_copy(way, h).wait_recv()

            @pl.when(h + 1 < n_z)
            def _():
                for way in (0, 1):

                    @pl.when(line_sends(way, h + 1))
                    def _():
                        line_copy(way, h + 1).start()

            @pl.when(h < n_z)
            def _():
                @pl.when(z - h >= 0)
                def _():
                    spread_rows(z - h)

                @pl.when(jnp.logical_and(h > 0, z + h < n_z))
                def _():
                    spread_rows(z + h)

            @pl.when(h == n_z + 1)
            def _():
                lax.fori_loop(0, n_row * folds, keep_rows, 0)

        for d in (0, 1):
            depth = z if d == 0 else n_z - 1 - z
            i = s - 1 - SKEW * depth

            @pl.when(jnp.logical_and(i + 1 >= 0, i + 1 < n))
            def _():
                k = i + 1

                @pl.when(k >= SLOTS)
                def _():
                    give(d, k).wait_send()

                give_v[d, k % SLOTS] = product(1 - core, d, k)
                give(d, k).start()

            @pl.when(jnp.logical_and(i >= 0, i < n))
            def _():
                mine = product(core, d, i)
                give(d, i).wait_recv()
                pair_v[d, i] = mine + pair_v[d, i]

                def onward():
                    return remote(
                        chain_v.at[d, i], chain_v.at[d, i], chain_send.at[d],
                        chain_recv.at[d, i], {"col": col + (-2 if d else 2)},
                    )

                @pl.when(depth == 0)
                def _():
                    chain_v[d, i] = pair_v[d, i]

                @pl.when(depth > 0)
                def _():
                    onward().wait_recv()
                    chain_v[d, i] = chain_v[d, i] + pair_v[d, i]

                @pl.when(depth < n_z - 1)
                def _():
                    onward().start()

                @pl.when(depth == n_z - 1)
                def _():
                    done_v[d, i] = chain_v[d, i].astype(done_v.dtype)
                    back(d, i).start()
                    arrived(d, i)

            away = n_z - 1 - depth
            g = s - 1 - SKEW * (n_z - 1) - SKEW * away

            @pl.when(jnp.logical_and(away > 0, jnp.logical_and(g >= 0, g < n)))
            def _():
                back(d, g).wait_recv()

                @pl.when(away < n_z - 1)
                def _():
                    back(d, g).start()

                arrived(d, g)

            x = g - MIRROR_LAG * hop

            @pl.when(
                jnp.logical_and(
                    jnp.logical_and(hop > 0, mirrored(x)), jnp.logical_and(x >= 0, x < n)
                )
            )
            def _():
                part = mir_v.at[d, x]
                remote(part, part, mir_send, mir_recv.at[d, x], next_row).wait_recv()
                mirror_copy(d, x, part)

        return 0

    steps = n + 1 + 2 * SKEW * (n_z - 1) + MIRROR_LAG * (n_row - 1)
    lax.fori_loop(0, steps, step, 0)

    lax.fori_loop(0, n_z, spread_wait, 0)
    pltpu.make_async_copy(rr_v, rr_v, rr_own).wait()
    remote(rr_v, rr_v, half_send, half_recv, sib).wait()
    pltpu.make_async_copy(mirror, mirror, mir_own).wait()

    @pl.when(hop < n_row - 1)
    def _():
        remote(mirror, mirror, mir_send, mir_recv.at[0, 0], sib).wait_send()

    own_rc.wait()
    for h in range(1, n_row):
        left_copy(h).wait_send()
        rc_copy(h).wait()

    def line_wait(h, _):
        for way in (0, 1):

            @pl.when(line_sends(way, h))
            def _():
                line_copy(way, h).wait_send()

        return 0

    lax.fori_loop(1, n_z, line_wait, 0)
    for d in (0, 1):
        depth = z if d == 0 else n_z - 1 - z
        pltpu.make_async_copy(done_v.at[d], done_v.at[d], done_sem.at[d]).wait()
        remote(done_v.at[d], done_v.at[d], fit_send.at[d], fit_recv.at[d], sib).wait()
        for k in range(n - SLOTS, n):
            give(d, k).wait_send()

        @pl.when(depth < n_z - 1)
        def _():
            remote(
                chain_v.at[d], chain_v.at[d], chain_send.at[d], chain_recv.at[d, 0], sib
            ).wait_send()

        @pl.when(depth > 0)
        def _():
            remote(
                done_v.at[d], done_v.at[d], back_send.at[d], back_recv.at[d, 0], sib
            ).wait_send()


def gather_all(amplitudes, aux_left, aux_right):
    n_row, n_col = lax.axis_size("row"), lax.axis_size("col")
    rows_here, cols_here = amplitudes.shape
    aux_block = aux_left.shape[1]
    aux = aux_block * n_row
    folds = n_col // n_row // 2
    n_z = n_col // 2
    tile = min(TILE, cols_here // 2)
    n = n_row * (rows_here // 4 // tile)
    dma = pltpu.SemaphoreType.DMA
    anywhere = pl.BlockSpec(memory_space=pl.ANY)
    low = amplitudes.dtype
    shapes = [
        (n_row, rows_here, aux_block), (n_row, cols_here, aux_block),
        (n_row, cols_here, aux_block), (n_row, rows_here, aux_block),
    ]
    return pl.pallas_call(
        functools.partial(gather_kernel, n_row, n_col),
        out_shape=[jax.ShapeDtypeStruct(s, low) for s in shapes],
        in_specs=[anywhere] * 3,
        out_specs=[anywhere] * 4,
        scratch_shapes=[
            pltpu.VMEM((rows_here, cols_here), low),
            pltpu.VMEM((n_row, cols_here, aux_block), low),
            pltpu.VMEM((2, n, tile, aux_block), jnp.float32),
            pltpu.VMEM((2, n, tile, aux_block), jnp.float32),
            pltpu.VMEM((2, SLOTS, tile, aux_block), jnp.float32),
            pltpu.VMEM((2, n, tile, aux_block), low),
            pltpu.VMEM((n_z, cols_here, aux_block), low),
            pltpu.VMEM((n_row, folds, cols_here, aux_block), low),
            pltpu.VMEM((2, n, tile, aux_block), low),
            dma(()), dma((3,)), dma((n_row,)), dma((n_row,)), dma((n_row,)), dma((n_row,)),
            dma((2,)), dma((2, n)), dma((2, SLOTS)), dma((2, n)),
            dma((2,)), dma((2, n)), dma((2,)), dma((2,)), dma((2,)),
            dma(()), dma((2, n)), dma(()),
            dma((2, n_z)), dma((2, n_z)), dma((n_z,)), dma((n_row * folds,)),
            dma(()), dma(()), dma(()),
        ],
        compiler_params=pltpu.CompilerParams(
            collective_id=0, has_side_effects=True, vmem_limit_bytes=60 * 2**20
        ),
        cost_estimate=pl.CostEstimate(
            flops=2 * rows_here * cols_here * aux, bytes_accessed=2 * rows_here * cols_here,
            transcendentals=0,
        ),
        name="gather_all",
    )(amplitudes, aux_left, aux_right)


def finish_kernel(fitted, right_rows, right_cols, mirror, row_gap, col_gap, out, held):
    blocks = range(fitted.shape[0])

    @pl.when(pl.program_id(0) == 0)
    def _():
        held[...] = jnp.concatenate(
            [right_cols[j] for j in blocks] + [mirror[j] for j in blocks], axis=1
        )

    rows = jnp.concatenate([fitted[j] for j in blocks] + [right_rows[j] for j in blocks], axis=1)
    total = lax.dot_general(
        rows, held[...], (((1,), (1,)), ((), ())), preferred_element_type=jnp.float32
    )
    out[...] = total / (row_gap[...] + col_gap[...])


def finish(fitted, right_rows, right_cols, mirror, row_gap, col_gap):
    n_row, rows_here, aux_block = fitted.shape
    cols_here = mirror.shape[1]
    tile = min(512, rows_here)
    by_row = pl.BlockSpec((n_row, tile, aux_block), lambda i: (0, i, 0))
    whole = pl.BlockSpec((n_row, cols_here, aux_block), lambda i: (0, 0, 0))
    return pl.pallas_call(
        finish_kernel,
        grid=(rows_here // tile,),
        out_shape=jax.ShapeDtypeStruct((rows_here, cols_here), jnp.float32),
        in_specs=[
            by_row, by_row, whole, whole,
            pl.BlockSpec((tile, 1), lambda i: (i, 0)),
            pl.BlockSpec((1, cols_here), lambda i: (0, 0)),
        ],
        out_specs=pl.BlockSpec((tile, cols_here), lambda i: (i, 0)),
        scratch_shapes=[pltpu.VMEM((cols_here, 2 * n_row * aux_block), fitted.dtype)],
        compiler_params=pltpu.CompilerParams(vmem_limit_bytes=52 * 2**20),
        name="finish",
    )(fitted, right_rows, right_cols, mirror, row_gap, col_gap)


def per_device(
    amplitudes, aux_left, aux_right, occupied_map, virtual_map, occupied_energy, virtual_energy
):
    rows_here, cols_here = amplitudes.shape
    gap = functools.partial(pair_gap, occupied_map, virtual_map, occupied_energy, virtual_energy)
    row_gap = gap(lax.axis_index("row") * rows_here, rows_here)
    col_gap = gap(lax.axis_index("col") * cols_here, cols_here)
    fitted, mirror, right_cols, right_rows = gather_all(amplitudes, aux_left, aux_right)
    return finish(
        fitted, right_rows, right_cols, mirror, row_gap[:, None], col_gap[None, :]
    )


def solution(mesh):
    return jax.shard_map(
        per_device,
        mesh=mesh,
        in_specs=(P("row", "col"), P("col", "row"), P("col", "row"), P(), P(), P(), P()),
        out_specs=P("row", "col"),
        check_vma=False,
    )
```

```python
import functools

import jax
import jax.numpy as jnp
from jax import lax
from jax.experimental import pallas as pl
from jax.experimental.pallas import tpu as pltpu
from jax.sharding import PartitionSpec as P

MESH = pl.DeviceIdType.MESH
SKEW = 3
HOP = 8
MIRROR_LAG = 10
BACK_LAG = 4
RING_LAG = 8
SLOTS = 8
TILE = 128


def lookup(positions, energies):
    shape = (energies.shape[0], positions.shape[1])
    matches = lax.broadcasted_iota(jnp.int32, shape, 0) == positions
    return jnp.sum(jnp.where(matches, energies, 0.0), axis=0, keepdims=True)


def gather_kernel(
    n_row, n_col, amp, left, right,
    fitted, mirror, right_cols, right_rows,
    amp_v, left_v, chain_v, pair_v, give_v, done_v, line_v, rr_v, mir_v,
    amp_sem, own_sem, left_send, left_recv, rc_send, rc_recv,
    chain_send, chain_recv, pair_send, pair_recv,
    back_send, back_recv, done_sem, fit_send, fit_recv,
    mir_send, mir_recv, mir_own,
    line_send, line_recv, rr_send, rr_recv, rr_own, half_send, half_recv,
):
    rows_here, cols_here = amp.shape
    fold = n_col // n_row
    folds = fold // 2
    n_z = n_col // 2
    tile = chain_v.shape[2]
    per_sub = cols_here // 2 // tile
    n_t = folds * per_sub
    n = n_row * n_t
    row = lax.axis_index("row")
    col = lax.axis_index("col")
    z = col // 2
    core = col % 2
    sib = {"col": col + 1 - 2 * core}
    owner = (col // fold) == row

    def remote(src, dst, send, recv, where):
        return pltpu.make_async_remote_copy(
            src_ref=src, dst_ref=dst, send_sem=send, recv_sem=recv,
            device_id=where, device_id_type=MESH,
        )

    def peer(b):
        return {"row": (row - b + n_row) % n_row}

    def ring(p):
        turn = p // (n_row // 2)
        return (1 - turn) * p + turn * (n_row - 1 - p + n_row // 2)

    spot = ring(row)
    way_round = 1 - 2 * core
    next_row = {"row": ring((spot + way_round + n_row) % n_row)}
    owner_spot = ring(col // fold)
    hop = ((spot - owner_spot) * way_round + n_row) % n_row

    def behind(h):
        return ring((spot - h * way_round + h * n_row) % n_row)

    def aux_at(place, i):
        b = i // n_t
        moved = (b + n_row - 1) // n_row
        offset = moved * (n_row // 2 + (b // 2) * (2 * (b % 2) - 1))
        return ring((place + offset) % n_row)

    def start_row(m, d, t):
        return pl.multiple_of(
            (2 * (t // per_sub) + m) * cols_here + d * (cols_here // 2) + (t % per_sub) * tile, tile
        )

    barrier = pltpu.get_barrier_semaphore()
    pl.semaphore_signal(barrier, inc=1, device_id=sib, device_id_type=MESH)
    for b in range(1, n_row):
        pl.semaphore_signal(barrier, inc=1, device_id=peer(b), device_id_type=MESH)

    @pl.when(z > 0)
    def _():
        pl.semaphore_signal(barrier, inc=1, device_id={"col": col - 2}, device_id_type=MESH)

    @pl.when(z < n_z - 1)
    def _():
        pl.semaphore_signal(barrier, inc=1, device_id={"col": col + 2}, device_id_type=MESH)

    amp_copy = pltpu.make_async_copy(amp, amp_v, amp_sem)
    amp_copy.start()
    own_left = pltpu.make_async_copy(left, left_v.at[row], own_sem.at[0])
    own_left.start()
    own_line = pltpu.make_async_copy(right, line_v.at[z], own_sem.at[1])
    own_line.start()

    line_ends = (z + n_z - 1) // n_z + (2 * (n_z - 1) - z) // n_z
    pl.semaphore_wait(barrier, n_row + line_ends)

    def left_copy(h):
        block = left_v.at[behind(h - 1)]
        return remote(block, block, left_send.at[h], left_recv.at[h], next_row)

    def rc_copy(b):
        return remote(
            line_v.at[z], right_cols.at[row], rc_send.at[b], rc_recv.at[b], peer(b)
        )

    own_left.wait()
    left_copy(1).start()
    own_line.wait()
    own_rc = pltpu.make_async_copy(line_v.at[z], right_cols.at[row], own_sem.at[2])
    own_rc.start()
    amp_copy.wait()

    def product(m, d, i):
        j = aux_at(spot, i)
        rows = amp_v[pl.ds(start_row(m, d, i % n_t), tile), :]
        return jnp.dot(rows, left_v[j], preferred_element_type=jnp.float32)

    def place(d, i):
        j = aux_at(spot, i)
        return (j, pl.ds(start_row(core, d, i % n_t), tile))

    def mirrored(i):
        return (i % n_t) // per_sub == (col % fold) // 2

    def mirror_copy(d, i, src):
        t = i % n_t
        at = pl.multiple_of(d * (cols_here // 2) + (t % per_sub) * tile, tile)
        target = mirror.at[aux_at(owner_spot, i), pl.ds(at, tile)]
        pltpu.make_async_copy(src, target, mir_own).start()

        @pl.when(hop < n_row - 1)
        def _():
            remote(src, mir_v.at[d, i], mir_send, mir_recv.at[d, i], next_row).start()

    def arrived(d, i):
        chunk = done_v.at[d, i]
        block, rows = place(d, i)
        target = fitted.at[block, rows]
        remote(chunk, target, fit_send.at[d], fit_recv.at[d], sib).start()
        pltpu.make_async_copy(chunk, target, done_sem.at[d]).start()

        @pl.when(jnp.logical_and(owner, mirrored(i)))
        def _():
            mirror_copy(d, i, chunk)

    def back(d, i):
        chunk = done_v.at[d, i]
        return remote(
            chunk, chunk, back_send.at[d], back_recv.at[d, i], {"col": col + (2 if d else -2)}
        )

    def line_copy(way, h):
        block = z - h + 1 if way == 0 else z + h - 1
        return remote(
            line_v.at[block], line_v.at[block], line_send.at[way, h], line_recv.at[way, h],
            {"col": col + (2 if way == 0 else -2)},
        )

    def line_sends(way, h):
        if way == 0:
            return jnp.logical_and(z + 1 < n_z, z - h + 1 >= 0)
        return jnp.logical_and(z >= 1, z + h - 1 < n_z)

    def line_gets(way, h):
        return z - h >= 0 if way == 0 else z + h < n_z

    def rows_of(block):
        block_col = 2 * block + core
        dest = block_col // fold
        part = (block_col % fold) // 2
        return dest, remote(
            line_v.at[block], rr_v.at[row, part], rr_send.at[block],
            rr_recv.at[row * folds + part], {"row": dest},
        )

    def spread_rows(block):
        dest, copy = rows_of(block)

        @pl.when(dest != row)
        def _():
            copy.start()

    def spread_wait(block, _):
        dest, copy = rows_of(block)

        @pl.when(dest != row)
        def _():
            copy.wait_send()

        return 0

    def keep_rows(k, _):
        source = k // folds
        part = k % folds
        at = pl.multiple_of((2 * part + core) * cols_here, cols_here)
        target = right_rows.at[source, pl.ds(at, cols_here)]

        def keep(src):
            pltpu.make_async_copy(src, target, rr_own).start()
            remote(src, target, half_send, half_recv, sib).start()

        @pl.when(source == row)
        def _():
            keep(line_v.at[row * folds + part])

        @pl.when(source != row)
        def _():
            here = rr_v.at[source, part]
            remote(here, here, rr_send.at[0], rr_recv.at[k], sib).wait_recv()
            keep(here)

        return 0

    def give(d, k):
        return remote(
            give_v.at[d, k % SLOTS], pair_v.at[d, k], pair_send.at[d, k % SLOTS],
            pair_recv.at[d, k], sib,
        )

    def step(s, _):
        half_way = n_row // 2
        for h in range(1, n_row):
            left_at = (n_t - 1) * h // half_way if h <= half_way else 2 * (h - half_way) * n_t - 1

            @pl.when(s == left_at)
            def _():
                left_copy(h).wait_recv()
                if h + 1 < n_row:
                    left_copy(h + 1).start()

            @pl.when(s == half_way * n_t + RING_LAG * (h - 2) + 2)
            def _():
                rc_copy(h).start()

        @pl.when(s % HOP == 0)
        def _():
            h = s // HOP

            @pl.when(jnp.logical_and(h >= 1, h < n_z))
            def _():
                for way in (0, 1):

                    @pl.when(line_gets(way, h))
                    def _():
                        line_copy(way, h).wait_recv()

            @pl.when(h + 1 < n_z)
            def _():
                for way in (0, 1):

                    @pl.when(line_sends(way, h + 1))
                    def _():
                        line_copy(way, h + 1).start()

            @pl.when(h < n_z)
            def _():
                @pl.when(z - h >= 0)
                def _():
                    spread_rows(z - h)

                @pl.when(jnp.logical_and(h > 0, z + h < n_z))
                def _():
                    spread_rows(z + h)

            @pl.when(h == n_z + 1)
            def _():
                lax.fori_loop(0, n_row * folds, keep_rows, 0)

        for d in (0, 1):
            depth = z if d == 0 else n_z - 1 - z
            i = s - 1 - SKEW * depth

            @pl.when(jnp.logical_and(i + 1 >= 0, i + 1 < n))
            def _():
                k = i + 1

                @pl.when(k >= SLOTS)
                def _():
                    give(d, k).wait_send()

                give_v[d, k % SLOTS] = product(1 - core, d, k)
                give(d, k).start()

            @pl.when(jnp.logical_and(i >= 0, i < n))
            def _():
                mine = product(core, d, i)
                give(d, i).wait_recv()
                pair_v[d, i] = mine + pair_v[d, i]

                def onward():
                    return remote(
                        chain_v.at[d, i], chain_v.at[d, i], chain_send.at[d],
                        chain_recv.at[d, i], {"col": col + (-2 if d else 2)},
                    )

                @pl.when(depth == 0)
                def _():
                    chain_v[d, i] = pair_v[d, i]

                @pl.when(depth > 0)
                def _():
                    onward().wait_recv()
                    chain_v[d, i] = chain_v[d, i] + pair_v[d, i]

                @pl.when(depth < n_z - 1)
                def _():
                    onward().start()

                @pl.when(depth == n_z - 1)
                def _():
                    done_v[d, i] = chain_v[d, i].astype(done_v.dtype)
                    back(d, i).start()
                    arrived(d, i)

            away = n_z - 1 - depth
            g = s - 1 - SKEW * (n_z - 1) - BACK_LAG * away

            @pl.when(jnp.logical_and(away > 0, jnp.logical_and(g >= 0, g < n)))
            def _():
                back(d, g).wait_recv()

                @pl.when(away < n_z - 1)
                def _():
                    back(d, g).start()

                arrived(d, g)

            x = g - MIRROR_LAG * hop

            @pl.when(
                jnp.logical_and(
                    jnp.logical_and(hop > 0, mirrored(x)), jnp.logical_and(x >= 0, x < n)
                )
            )
            def _():
                part = mir_v.at[d, x]
                remote(part, part, mir_send, mir_recv.at[d, x], next_row).wait_recv()
                mirror_copy(d, x, part)

        return 0

    steps = n + 1 + (SKEW + BACK_LAG) * (n_z - 1) + MIRROR_LAG * (n_row - 1)
    lax.fori_loop(0, steps, step, 0)

    lax.fori_loop(0, n_z, spread_wait, 0)
    pltpu.make_async_copy(rr_v, rr_v, rr_own).wait()
    remote(rr_v, rr_v, half_send, half_recv, sib).wait()
    pltpu.make_async_copy(mirror, mirror, mir_own).wait()

    @pl.when(hop < n_row - 1)
    def _():
        remote(mirror, mirror, mir_send, mir_recv.at[0, 0], sib).wait_send()

    own_rc.wait()
    for h in range(1, n_row):
        left_copy(h).wait_send()
        rc_copy(h).wait()

    def line_wait(h, _):
        for way in (0, 1):

            @pl.when(line_sends(way, h))
            def _():
                line_copy(way, h).wait_send()

        return 0

    lax.fori_loop(1, n_z, line_wait, 0)
    for d in (0, 1):
        depth = z if d == 0 else n_z - 1 - z
        pltpu.make_async_copy(done_v.at[d], done_v.at[d], done_sem.at[d]).wait()
        remote(done_v.at[d], done_v.at[d], fit_send.at[d], fit_recv.at[d], sib).wait()
        for k in range(n - SLOTS, n):
            give(d, k).wait_send()

        @pl.when(depth < n_z - 1)
        def _():
            remote(
                chain_v.at[d], chain_v.at[d], chain_send.at[d], chain_recv.at[d, 0], sib
            ).wait_send()

        @pl.when(depth > 0)
        def _():
            remote(
                done_v.at[d], done_v.at[d], back_send.at[d], back_recv.at[d, 0], sib
            ).wait_send()


def gather_all(amplitudes, aux_left, aux_right):
    n_row, n_col = lax.axis_size("row"), lax.axis_size("col")
    rows_here, cols_here = amplitudes.shape
    aux_block = aux_left.shape[1]
    aux = aux_block * n_row
    folds = n_col // n_row // 2
    n_z = n_col // 2
    tile = min(TILE, cols_here // 2)
    n = n_row * (rows_here // 4 // tile)
    dma = pltpu.SemaphoreType.DMA
    anywhere = pl.BlockSpec(memory_space=pl.ANY)
    low = amplitudes.dtype
    shapes = [
        (n_row, rows_here, aux_block), (n_row, cols_here, aux_block),
        (n_row, cols_here, aux_block), (n_row, rows_here, aux_block),
    ]
    return pl.pallas_call(
        functools.partial(gather_kernel, n_row, n_col),
        out_shape=[jax.ShapeDtypeStruct(s, low) for s in shapes],
        in_specs=[anywhere] * 3,
        out_specs=[anywhere] * 4,
        scratch_shapes=[
            pltpu.VMEM((rows_here, cols_here), low),
            pltpu.VMEM((n_row, cols_here, aux_block), low),
            pltpu.VMEM((2, n, tile, aux_block), jnp.float32),
            pltpu.VMEM((2, n, tile, aux_block), jnp.float32),
            pltpu.VMEM((2, SLOTS, tile, aux_block), jnp.float32),
            pltpu.VMEM((2, n, tile, aux_block), low),
            pltpu.VMEM((n_z, cols_here, aux_block), low),
            pltpu.VMEM((n_row, folds, cols_here, aux_block), low),
            pltpu.VMEM((2, n, tile, aux_block), low),
            dma(()), dma((3,)), dma((n_row,)), dma((n_row,)), dma((n_row,)), dma((n_row,)),
            dma((2,)), dma((2, n)), dma((2, SLOTS)), dma((2, n)),
            dma((2,)), dma((2, n)), dma((2,)), dma((2,)), dma((2,)),
            dma(()), dma((2, n)), dma(()),
            dma((2, n_z)), dma((2, n_z)), dma((n_z,)), dma((n_row * folds,)),
            dma(()), dma(()), dma(()),
        ],
        compiler_params=pltpu.CompilerParams(
            collective_id=0, has_side_effects=True, vmem_limit_bytes=60 * 2**20
        ),
        cost_estimate=pl.CostEstimate(
            flops=2 * rows_here * cols_here * aux, bytes_accessed=2 * rows_here * cols_here,
            transcendentals=0,
        ),
        name="gather_all",
    )(amplitudes, aux_left, aux_right)


def finish_kernel(
    fitted, right_rows, right_cols, mirror, row_occ, row_virt, col_occ, col_virt,
    occ_energy, virt_energy, out, held, col_gap,
):
    blocks = range(fitted.shape[0])

    @pl.when(pl.program_id(0) == 0)
    def _():
        held[...] = jnp.concatenate(
            [right_cols[j] for j in blocks] + [mirror[j] for j in blocks], axis=1
        )
        col_gap[...] = lookup(col_virt[...], virt_energy[...]) - lookup(
            col_occ[...], occ_energy[...]
        )

    rows = jnp.concatenate([fitted[j] for j in blocks] + [right_rows[j] for j in blocks], axis=1)
    total = lax.dot_general(
        rows, held[...], (((1,), (1,)), ((), ())), preferred_element_type=jnp.float32
    )
    row_gap = lookup(row_virt[...], virt_energy[...]) - lookup(row_occ[...], occ_energy[...])
    down = jnp.transpose(jnp.broadcast_to(row_gap, (128, row_gap.shape[1])))[:, :1]
    out[...] = total / (down + col_gap[...])


def finish(
    fitted, right_rows, right_cols, mirror, occupied_map, virtual_map, occupied_energy,
    virtual_energy,
):
    n_row, rows_here, aux_block = fitted.shape
    cols_here = mirror.shape[1]
    tile = min(512, rows_here)
    steps = rows_here // tile
    occ, virt = occupied_map[None, :], virtual_map[None, :]
    occ_energy, virt_energy = occupied_energy[:, None], virtual_energy[:, None]
    row_map = pl.BlockSpec((1, tile), lambda i: (0, lax.axis_index("row") * steps + i))
    col_map = pl.BlockSpec((1, cols_here), lambda i: (0, lax.axis_index("col")))
    by_row = pl.BlockSpec((n_row, tile, aux_block), lambda i: (0, i, 0))
    whole = pl.BlockSpec((n_row, cols_here, aux_block), lambda i: (0, 0, 0))
    return pl.pallas_call(
        finish_kernel,
        grid=(rows_here // tile,),
        out_shape=jax.ShapeDtypeStruct((rows_here, cols_here), jnp.float32),
        in_specs=[
            by_row, by_row, whole, whole,
            row_map, row_map, col_map, col_map,
            pl.BlockSpec(occ_energy.shape, lambda i: (0, 0)),
            pl.BlockSpec(virt_energy.shape, lambda i: (0, 0)),
        ],
        out_specs=pl.BlockSpec((tile, cols_here), lambda i: (i, 0)),
        scratch_shapes=[
            pltpu.VMEM((cols_here, 2 * n_row * aux_block), fitted.dtype),
            pltpu.VMEM((1, cols_here), jnp.float32),
        ],
        compiler_params=pltpu.CompilerParams(vmem_limit_bytes=52 * 2**20),
        name="finish",
    )(
        fitted, right_rows, right_cols, mirror, occ, virt, occ, virt, occ_energy, virt_energy
    )


def per_device(
    amplitudes, aux_left, aux_right, occupied_map, virtual_map, occupied_energy, virtual_energy
):
    fitted, mirror, right_cols, right_rows = gather_all(amplitudes, aux_left, aux_right)
    return finish(
        fitted, right_rows, right_cols, mirror, occupied_map, virtual_map, occupied_energy,
        virtual_energy,
    )


def solution(mesh):
    return jax.shard_map(
        per_device,
        mesh=mesh,
        in_specs=(P("row", "col"), P("col", "row"), P("col", "row"), P(), P(), P(), P()),
        out_specs=P("row", "col"),
        check_vma=False,
    )
```
